32 devices in a mesh: tiles: 16 (over z, y, x), rep: 2 (over core).
Axes of the slice: x: 2, y: 2, z: 4, core: 2. Of those that a mesh axis runs over, the one named last changes fastest.
Arguments:
- members: bfloat16 [512, 80, 256], P(('tiles', 'rep')), may hold values from -1350 to 1350
- initial: bfloat16 [512, 32, 256], P(('tiles', 'rep')), may hold values from -6 to 6
- wet_counts: int32 [512], P(('tiles', 'rep')), may hold values from 1 to 256, as said below
- tile_coords: int32 [512, 2], P(('tiles', 'rep')), may hold values from 0 to 63, as said below
- neighbours: int32 [512, 9], P(('tiles', 'rep')), may hold values from -1 to 511, as said below
Outputs:
- leading: float32 [512, 32, 256], P(('tiles', 'rep'))
The draws below stay inside these ranges and needn't reach their ends.
Inputs may be any that keep to these rules, and one draw needn't show every extreme that they name: `wet_counts`: each tile's count of wet points; some tiles are all wet. `tile_coords`: tiles form a strip of columns of 8 consecutive tiles; the first entry is the column, consecutive columns are offset by at most one tile in the second entry. `neighbours`: each tile lists, in increasing order and followed by -1 padding, every tile whose two entries of tile_coords differ from its own by at most one, itself included; the list is symmetric.
All inputs are finite; a program needn't handle non-finite values.
Results may differ from the reference program's by a relative error of at most 0.00065.
The reference program's roundings to bfloat16 on the way count: a program that leaves them out, or rounds other values in their place, can miss the bound.
Values may be sent and summed in bfloat16 or wider, within the bound.
A program may use at most 128 MiB of HBM per device.

```python
import math
import jax
import jax.numpy as jnp
from jax import lax

TILE_SIDE = 16
GRID_POINTS = 256
MEMBERS = 80
RANK = 32
NBR = 9
COLW = 8
ITERS = 2
TILE_TOTAL = 512


def tile_layout(key):
    column_count = TILE_TOTAL // COLW
    layout_key = jax.random.fold_in(key, 101)
    column_ids = jnp.arange(column_count, dtype=jnp.int32)
    drawn_shift = jax.random.randint(layout_key, (column_count,), 0, 2, dtype=jnp.int32)
    shifts = jnp.where(column_ids == 0, 1, jnp.where(column_ids == 1, 0, drawn_shift)).astype(jnp.int32)
    tile_ids = jnp.arange(TILE_TOTAL, dtype=jnp.int32)
    across = tile_ids // COLW
    upward = tile_ids % COLW + shifts[across]
    places = jnp.stack([across, upward], axis=1)
    offsets = jnp.arange(-(COLW + 2), COLW + 3, dtype=jnp.int32)
    candidate = tile_ids[:, None] + offsets[None, :]
    inside = (candidate >= 0) & (candidate < TILE_TOTAL)
    clipped = jnp.clip(candidate, 0, TILE_TOTAL - 1)
    adjacent = inside & (jnp.abs(across[clipped] - across[:, None]) <= 1) & (jnp.abs(upward[clipped] - upward[:, None]) <= 1)
    position = jnp.cumsum(adjacent.astype(jnp.int32), axis=1) - 1
    position = jnp.where(adjacent, position, NBR)
    neighbour_lists = jnp.full((TILE_TOTAL, NBR), -1, dtype=jnp.int32)
    neighbour_lists = neighbour_lists.at[tile_ids[:, None], position].set(candidate, mode='drop')
    return (places, neighbour_lists)


def draw_tile_coords(key, part):
    return tile_layout(key)[0]


def draw_neighbours(key, part):
    return tile_layout(key)[1]


def draw_wet_counts(key, part):
    point_counts = jax.random.randint(jax.random.fold_in(key, 5), (TILE_TOTAL,), 1, GRID_POINTS + 1, dtype=jnp.int32)
    open_ocean = jax.random.randint(jax.random.fold_in(key, 6), (TILE_TOTAL,), 0, 3, dtype=jnp.int32) == 0
    tile_ids = jnp.arange(TILE_TOTAL, dtype=jnp.int32)
    return jnp.where(open_ocean | (tile_ids % 5 == 0), GRID_POINTS, point_counts).astype(jnp.int32)


def draw_members(key, part):
    perturb = jnp.clip(jax.random.normal(jax.random.fold_in(key, 1), (TILE_TOTAL, MEMBERS, GRID_POINTS), jnp.float32), -4.0, 4.0)
    tile_scale = jnp.exp(jax.random.uniform(jax.random.fold_in(key, 2), (TILE_TOTAL, 1, 1), jnp.float32, 0.0, math.log(10.0)))
    tile_ids = jnp.arange(TILE_TOTAL, dtype=jnp.int32)
    growth = (1.0 + 2.0 * tile_ids.astype(jnp.float32) / max(TILE_TOTAL - 1, 1)).reshape(TILE_TOTAL, 1, 1)
    rim_tiles = (tile_ids < 3 * COLW) | (tile_ids >= TILE_TOTAL - 3 * COLW)
    edge_boost = jnp.where(rim_tiles, 3.0, 1.0).astype(jnp.float32).reshape(TILE_TOTAL, 1, 1)
    return (perturb * tile_scale * growth * edge_boost).astype(jnp.bfloat16)


def levels(stream_key, extent, pieces, smallest, high):
    def one(axis_at, shards_of):
        heights = jax.random.uniform(jax.random.fold_in(jax.random.fold_in(stream_key, 6), axis_at), (shards_of,), jnp.float32, smallest / len(pieces), high / len(pieces))
        return jnp.repeat(jnp.exp(heights), extent[axis_at] // shards_of).reshape((-1,) + (1,) * (len(extent) - axis_at - 1))

    loudness = one(*pieces[0])
    for cut in pieces[1:]:
        loudness = loudness * one(*cut)
    return loudness


def bell_draw(stream_key, dims, deviation, reach, shards=(), kind=jnp.bfloat16):
    array = deviation * jax.random.normal(stream_key, dims, jnp.float32)
    if shards:
        array = array * levels(stream_key, dims, shards, -0.22, 0.18)
    return jnp.clip(array, -reach, reach).astype(kind)


def setup_inputs(seed: int = 0) -> dict:
    seeds = jax.random.split(jax.random.key(seed), 6)
    members = draw_members(jax.random.fold_in(seeds[5], 71), 0)
    initial = bell_draw(seeds[1], (TILE_TOTAL, RANK, GRID_POINTS), 1.0, 6.0, ((0, 32),))
    wet_counts = draw_wet_counts(jax.random.fold_in(seeds[5], 71), 0)
    tile_coords = draw_tile_coords(jax.random.fold_in(seeds[5], 71), 0)
    neighbours = draw_neighbours(jax.random.fold_in(seeds[5], 71), 0)
    return {"members": members, "initial": initial, "wet_counts": wet_counts, "tile_coords": tile_coords, "neighbours": neighbours}


def gaspari(distance):
    scaled = distance / (0.5 * TILE_SIDE)
    clamped = jnp.maximum(scaled, 1.0)
    inner_part = (((-0.25 * scaled + 0.5) * scaled + 0.625) * scaled - 5.0 / 3.0) * scaled * scaled + 1.0
    outer_part = ((((scaled / 12.0 - 0.5) * scaled + 0.625) * scaled + 5.0 / 3.0) * scaled - 5.0) * scaled + 4.0 - 2.0 / (3.0 * clamped)
    return jnp.where(scaled <= 1.0, inner_part, jnp.where(scaled <= 2.0, outer_part, 0.0))

def distances(place_one, place_two):
    points = jnp.arange(TILE_SIDE * TILE_SIDE, dtype=jnp.int32)
    across = points // TILE_SIDE
    along_row = points % TILE_SIDE
    row_one = place_one[..., 0:1] * TILE_SIDE + across
    col_one = place_one[..., 1:2] * TILE_SIDE + along_row
    row_two = place_two[..., 0:1] * TILE_SIDE + across
    col_two = place_two[..., 1:2] * TILE_SIDE + along_row
    delta_row = (row_one[..., :, None] - row_two[..., None, :]).astype(jnp.float32)
    delta_col = (col_one[..., :, None] - col_two[..., None, :]).astype(jnp.float32)
    return jnp.sqrt(delta_row * delta_row + delta_col * delta_col)

def covariance_apply(masked, tile_coords, neighbours, current):

    def one_tile(inputs):
        rows_one, place_one, listed = inputs
        usable = listed >= 0
        safe_index = jnp.maximum(listed, 0).astype(jnp.int32)
        product = jnp.einsum('mi,smj->sij', rows_one.astype(jnp.float32), masked[safe_index].astype(jnp.float32))
        weight = gaspari(distances(place_one[None, :], tile_coords[safe_index]))
        blocks = (product * weight / (MEMBERS - 1.0)).astype(jnp.bfloat16)
        contrib = jnp.einsum('skj,sij->ski', current[safe_index].astype(jnp.float32), blocks.astype(jnp.float32))
        return lax.optimization_barrier(jnp.sum(jnp.where(usable[:, None, None], contrib, 0.0), axis=0))
    return lax.map(one_tile, (masked, tile_coords, neighbours))

def orthonormal(applied_product):
    summed_gram = jnp.einsum('brg,bsg->rs', applied_product, applied_product, precision=lax.Precision.HIGHEST) / (TILE_TOTAL * GRID_POINTS * 1.0)
    factor = jnp.linalg.cholesky(summed_gram)
    inverse_factor = jax.scipy.linalg.solve_triangular(factor, jnp.eye(summed_gram.shape[0], dtype=jnp.float32), lower=True)
    return jnp.einsum('fy,ryc->rfc', inverse_factor, applied_product, precision=lax.Precision.HIGHEST)

def reference(members, initial, wet_counts, tile_coords, neighbours):
    wet_mask = jnp.arange(GRID_POINTS, dtype=jnp.int32)[None, :] < wet_counts[:, None]
    masked = jnp.where(wet_mask[:, None, :], members, jnp.zeros_like(members))
    current = initial
    fresh = jnp.zeros(initial.shape, jnp.float32)
    for sweep_index in range(ITERS):
        applied_product = covariance_apply(masked, tile_coords, neighbours, current)
        fresh = orthonormal(applied_product)
        current = fresh.astype(jnp.bfloat16)
    return fresh
```

```python
import functools

import jax
import jax.numpy as jnp
from jax import lax
from jax.experimental import pallas as pl
from jax.experimental.pallas import tpu as pltpu
from jax.sharding import PartitionSpec as P

TILE_SIDE = 16
COLW = 8
ITERS = 2
AXES = ("tiles", "rep")
HIGH = lax.Precision.HIGHEST


def from_behind(shard, by):
    length = lax.axis_size(AXES)
    pairs = [(i, i + by) for i in range(length) if 0 <= i + by < length]
    return lax.ppermute(shard, AXES, pairs)


def gaspari(distance):
    scaled = distance / (0.5 * TILE_SIDE)
    clamped = jnp.maximum(scaled, 1.0)
    inner_part = (
        ((-0.25 * scaled + 0.5) * scaled + 0.625) * scaled - 5.0 / 3.0
    ) * scaled * scaled + 1.0
    outer_part = (
        ((((scaled / 12.0 - 0.5) * scaled + 0.625) * scaled + 5.0 / 3.0) * scaled - 5.0) * scaled
        + 4.0
        - 2.0 / (3.0 * clamped)
    )
    return jnp.where(scaled <= 1.0, inner_part, jnp.where(scaled <= 2.0, outer_part, 0.0))


def taper_kernel(scale, table_ref):
    step = pl.program_id(0)
    points = table_ref.shape[1]
    delta_x = step // 3 - 1
    delta_y = step % 3 - 1
    one = lax.broadcasted_iota(jnp.int32, (points, points), 0)
    two = lax.broadcasted_iota(jnp.int32, (points, points), 1)
    row = (delta_x * TILE_SIDE + one // TILE_SIDE - two // TILE_SIDE).astype(jnp.float32)
    col = (delta_y * TILE_SIDE + one % TILE_SIDE - two % TILE_SIDE).astype(jnp.float32)
    weight = gaspari(jnp.sqrt(row * row + col * col)) * scale
    table_ref[0] = jnp.where(step == 9, 0.0, weight)


def taper_table(points, scale):
    return pl.pallas_call(
        functools.partial(taper_kernel, scale),
        grid=(10,),
        out_shape=jax.ShapeDtypeStruct((10, points, points), jnp.float32),
        out_specs=pl.BlockSpec((1, points, points), lambda i: (i, 0, 0)),
        cost_estimate=pl.CostEstimate(
            flops=10 * 40 * points * points, bytes_accessed=40 * points * points, transcendentals=0
        ),
    )()


def gram_add(step, applied, gram_ref):
    part = lax.dot_general(
        applied, applied, (((1,), (1,)), ((), ())), precision=HIGH, preferred_element_type=jnp.float32
    )

    @pl.when(step == 0)
    def _():
        gram_ref[...] = part

    @pl.when(step != 0)
    def _():
        gram_ref[...] += part


def first_kernel(slot_ref, kind_ref, turned_ref, own_ref, iter_ref, table_ref, blocks_ref, applied_ref, gram_ref):
    step = pl.program_id(0)
    own = own_ref[0]
    total = None
    for s in range(slot_ref.shape[1]):
        at = slot_ref[step, s]
        product = jnp.dot(turned_ref[at], own, preferred_element_type=jnp.float32)
        block = (product * table_ref[kind_ref[step, s]]).astype(jnp.bfloat16)
        blocks_ref[0, s] = block
        part = jnp.dot(iter_ref[at], block, preferred_element_type=jnp.float32)
        total = part if total is None else total + part
    applied_ref[0] = total
    gram_add(step, total, gram_ref)


def later_kernel(slot_ref, iter_ref, blocks_ref, applied_ref, gram_ref):
    step = pl.program_id(0)
    total = None
    for s in range(slot_ref.shape[1]):
        part = jnp.dot(iter_ref[slot_ref[step, s]], blocks_ref[0, s], preferred_element_type=jnp.float32)
        total = part if total is None else total + part
    applied_ref[0] = total
    gram_add(step, total, gram_ref)


def norm_kernel(total_points, gram_ref, applied_ref, fresh_ref):
    rank = gram_ref.shape[0]
    rows = lax.broadcasted_iota(jnp.int32, (rank, rank), 0)
    cols = lax.broadcasted_iota(jnp.int32, (rank, rank), 1)
    left = gram_ref[...] / total_points
    work = jnp.concatenate([left, (rows == cols).astype(jnp.float32)], axis=1)
    down = lax.broadcasted_iota(jnp.int32, (rank, 1), 0)
    for j in range(rank):
        root = lax.sqrt(work[j : j + 1, j : j + 1])
        line = work[j : j + 1, :] / root
        factor = work[:, j : j + 1] / root
        work = jnp.where(down > j, work - factor * line, jnp.where(down == j, line, work))
    inverse = work[:, rank:]
    for a in range(applied_ref.shape[0]):
        fresh_ref[a] = jnp.dot(
            inverse, applied_ref[a], precision=HIGH, preferred_element_type=jnp.float32
        ).astype(fresh_ref.dtype)


def whole(shape):
    return pl.BlockSpec(shape, lambda i: (0,) * len(shape))


def per_tile(shape):
    return pl.BlockSpec((1,) + tuple(shape[1:]), lambda i: (i,) + (0,) * (len(shape) - 1))


def smem():
    return pl.BlockSpec(memory_space=pltpu.SMEM)


PARAMS = pltpu.CompilerParams(vmem_limit_bytes=40 * 1024 * 1024)


def window(own, edge):
    ahead = from_behind(own[:edge], -1)
    behind = from_behind(own[-edge:], 1)
    return behind, ahead


def local(members, initial, wet_counts, tile_coords, neighbours):
    tiles, count, points = members.shape
    rank = initial.shape[1]
    slots = neighbours.shape[1]
    edge = COLW + 2
    first_tile = lax.axis_index(AXES) * tiles
    total_points = float(tiles * lax.axis_size(AXES) * points)
    wet_mask = jnp.arange(points, dtype=jnp.int32)[None, :] < wet_counts[:, None]
    own_rows = jnp.where(wet_mask[:, None, :], members, jnp.zeros_like(members))
    join = lambda own, sides: jnp.concatenate([sides[0], own, sides[1]], 0)
    rows = join(own_rows, window(own_rows, edge))
    place = join(tile_coords, window(tile_coords, edge))
    current = join(initial, window(initial, edge))
    slot = jnp.clip(neighbours - (first_tile - edge), 0, tiles + 2 * edge - 1)
    delta = jnp.clip(place[slot] - tile_coords[:, None, :], -1, 1) + 1
    kind = jnp.where(neighbours >= 0, delta[..., 0] * 3 + delta[..., 1], 9)
    table = taper_table(points, 1.0 / (count - 1.0))
    turned = jnp.swapaxes(rows, 1, 2)
    applied_shape = jax.ShapeDtypeStruct((tiles, rank, points), jnp.float32)
    gram_shape = jax.ShapeDtypeStruct((rank, rank), jnp.float32)
    blocks_shape = jax.ShapeDtypeStruct((tiles, slots, points, points), jnp.bfloat16)
    blocks, applied, gram = pl.pallas_call(
        first_kernel,
        grid=(tiles,),
        in_specs=[
            smem(), smem(), whole(turned.shape), per_tile(own_rows.shape), whole(current.shape), whole(table.shape),
        ],
        out_specs=[per_tile(blocks_shape.shape), per_tile(applied_shape.shape), whole(gram_shape.shape)],
        out_shape=[blocks_shape, applied_shape, gram_shape],
        compiler_params=PARAMS,
    )(slot, kind, turned, own_rows, current, table)
    for sweep in range(ITERS):
        gram = lax.psum(gram, AXES)
        last = sweep == ITERS - 1
        fresh = pl.pallas_call(
            functools.partial(norm_kernel, total_points),
            out_shape=jax.ShapeDtypeStruct(
                applied_shape.shape, jnp.float32 if last else jnp.bfloat16
            ),
            compiler_params=PARAMS,
        )(gram, applied)
        if last:
            return fresh
        current = join(fresh, window(fresh, edge))
        applied, gram = pl.pallas_call(
            later_kernel,
            grid=(tiles,),
            in_specs=[smem(), whole(current.shape), per_tile(blocks.shape)],
            out_specs=[per_tile(applied_shape.shape), whole(gram_shape.shape)],
            out_shape=[applied_shape, gram_shape],
            compiler_params=PARAMS,
        )(slot, current, blocks)


def solution(mesh):
    spec = P(AXES, None, None)
    in_specs = (spec, spec, P(AXES), P(AXES, None), P(AXES, None))
    return jax.shard_map(local, mesh=mesh, in_specs=in_specs, out_specs=spec, check_vma=False)
```

```python
import functools

import jax
import jax.numpy as jnp
from jax import lax
from jax.experimental import pallas as pl
from jax.experimental.pallas import tpu as pltpu
from jax.sharding import PartitionSpec as P

TILE_SIDE = 16
COLW = 8
ITERS = 2
AXES = ("tiles", "rep")
HIGH = lax.Precision.HIGHEST


def from_behind(shard, by):
    length = lax.axis_size(AXES)
    pairs = [(i, i + by) for i in range(length) if 0 <= i + by < length]
    return lax.ppermute(shard, AXES, pairs)


def gaspari(distance):
    scaled = distance / (0.5 * TILE_SIDE)
    clamped = jnp.maximum(scaled, 1.0)
    inner_part = (
        ((-0.25 * scaled + 0.5) * scaled + 0.625) * scaled - 5.0 / 3.0
    ) * scaled * scaled + 1.0
    outer_part = (
        ((((scaled / 12.0 - 0.5) * scaled + 0.625) * scaled + 5.0 / 3.0) * scaled - 5.0) * scaled
        + 4.0
        - 2.0 / (3.0 * clamped)
    )
    return jnp.where(scaled <= 1.0, inner_part, jnp.where(scaled <= 2.0, outer_part, 0.0))


def taper_kernel(scale, table_ref):
    step = pl.program_id(0)
    points = table_ref.shape[1]
    delta_x = step // 3 - 1
    delta_y = step % 3 - 1
    one = lax.broadcasted_iota(jnp.int32, (points, points), 0)
    two = lax.broadcasted_iota(jnp.int32, (points, points), 1)
    row = (delta_x * TILE_SIDE + one // TILE_SIDE - two // TILE_SIDE).astype(jnp.float32)
    col = (delta_y * TILE_SIDE + one % TILE_SIDE - two % TILE_SIDE).astype(jnp.float32)
    weight = gaspari(jnp.sqrt(row * row + col * col)) * scale
    table_ref[0] = jnp.where(step == 9, 0.0, weight)


def taper_table(points, scale):
    return pl.pallas_call(
        functools.partial(taper_kernel, scale),
        grid=(10,),
        out_shape=jax.ShapeDtypeStruct((10, points, points), jnp.float32),
        out_specs=pl.BlockSpec((1, points, points), lambda i: (i, 0, 0)),
        cost_estimate=pl.CostEstimate(
            flops=10 * 40 * points * points, bytes_accessed=40 * points * points, transcendentals=0
        ),
    )()


def gram_add(step, applied, gram_ref):
    part = lax.dot_general(
        applied, applied, (((1,), (1,)), ((), ())), precision=HIGH, preferred_element_type=jnp.float32
    )

    @pl.when(step == 0)
    def _():
        gram_ref[...] = part

    @pl.when(step != 0)
    def _():
        gram_ref[...] += part


def first_kernel(slot_ref, kind_ref, turned_ref, own_ref, iter_ref, table_ref, blocks_ref, applied_ref, gram_ref):
    step = pl.program_id(0)
    own = own_ref[0]
    total = None
    for s in range(slot_ref.shape[1]):
        at = slot_ref[step, s]
        product = jnp.dot(turned_ref[at], own, preferred_element_type=jnp.float32)
        block = (product * table_ref[kind_ref[step, s]]).astype(jnp.bfloat16)
        blocks_ref[0, s] = block
        part = jnp.dot(iter_ref[at], block, preferred_element_type=jnp.float32)
        total = part if total is None else total + part
    applied_ref[0] = total
    gram_add(step, total, gram_ref)


def later_kernel(slot_ref, iter_ref, blocks_ref, applied_ref, gram_ref):
    step = pl.program_id(0)
    total = None
    for s in range(slot_ref.shape[1]):
        part = jnp.dot(iter_ref[slot_ref[step, s]], blocks_ref[0, s], preferred_element_type=jnp.float32)
        total = part if total is None else total + part
    applied_ref[0] = total
    gram_add(step, total, gram_ref)


def device_at(index):
    width = lax.axis_size(AXES[1])
    return (index // width, index % width)


def digit_groups(length):
    groups = []
    stride = 1
    while stride < length:
        size = next(s for s in range(min(8, length // stride), 1, -1) if (length // stride) % s == 0)
        groups.append((stride, size))
        stride *= size
    return groups


def exchange(me, source, inbox, send_sem, recv_sem, groups):
    total = source[0]
    for phase, (stride, size) in enumerate(groups):
        digit = (me // stride) % size
        if phase:
            source[phase] = total
        inbox[phase, digit] = total
        copies = []
        for hop in range(1, size):
            other = me + ((digit + hop) % size - digit) * stride
            copy = pltpu.make_async_remote_copy(
                src_ref=source.at[phase],
                dst_ref=inbox.at[phase, digit],
                send_sem=send_sem.at[phase, hop],
                recv_sem=recv_sem.at[phase, hop],
                device_id=device_at(other),
                device_id_type=pl.DeviceIdType.MESH,
            )
            copy.start()
            copies.append(copy)
        for copy in copies:
            copy.wait()
        total = inbox[phase, 0]
        for at in range(1, size):
            total = total + inbox[phase, at]
    return total


def inverse_factor(left):
    rank = left.shape[0]
    rows = lax.broadcasted_iota(jnp.int32, (rank, rank), 0)
    cols = lax.broadcasted_iota(jnp.int32, (rank, rank), 1)
    work = jnp.concatenate([left, (rows == cols).astype(jnp.float32)], axis=1)
    down = lax.broadcasted_iota(jnp.int32, (rank, 1), 0)
    for j in range(rank):
        root = lax.sqrt(work[j : j + 1, j : j + 1])
        line = work[j : j + 1, :] / root
        factor = work[:, j : j + 1] / root
        work = jnp.where(down > j, work - factor * line, jnp.where(down == j, line, work))
    return work[:, rank:]


def norm_kernel(
    total_points, groups, edge, gram_ref, applied_ref, fresh_ref,
    source, inbox, halo, send_sem, recv_sem, halo_send, halo_recv,
):
    length = lax.axis_size(AXES)
    me = lax.axis_index(AXES[0]) * lax.axis_size(AXES[1]) + lax.axis_index(AXES[1])
    barrier = pltpu.get_barrier_semaphore()
    mesh_ids = pl.DeviceIdType.MESH
    greeted = 0
    for stride, size in groups:
        digit = (me // stride) % size
        for hop in range(1, size):
            other = me + ((digit + hop) % size - digit) * stride
            pl.semaphore_signal(barrier, inc=1, device_id=device_at(other), device_id_type=mesh_ids)
            greeted += 1
    sides = ((me > 0, -1), (me < length - 1, 1)) if edge else ()
    for there, by in sides:

        @pl.when(there)
        def _():
            pl.semaphore_signal(barrier, inc=1, device_id=device_at(me + by), device_id_type=mesh_ids)

    source[0] = gram_ref[...]
    if edge:
        greeted = greeted + jnp.minimum(me, 1) + jnp.minimum(length - 1 - me, 1)
    pl.semaphore_wait(barrier, greeted)

    inverse = inverse_factor(exchange(me, source, inbox, send_sem, recv_sem, groups) / total_points)
    tiles = applied_ref.shape[0]

    def put(a):
        fresh_ref[a + edge] = jnp.dot(
            inverse, applied_ref[a], precision=HIGH, preferred_element_type=jnp.float32
        ).astype(fresh_ref.dtype)

    if not edge:
        for a in range(tiles):
            put(a)
        return

    def shift(side):
        first = edge if side == 0 else tiles
        return pltpu.make_async_remote_copy(
            src_ref=fresh_ref.at[pl.ds(first, edge)],
            dst_ref=halo.at[1 - side],
            send_sem=halo_send.at[side],
            recv_sem=halo_recv.at[1 - side],
            device_id=device_at(me + sides[side][1]),
            device_id_type=mesh_ids,
        )

    for a in range(edge):
        put(a)
    pl.when(sides[0][0])(lambda: shift(0).start())
    for a in range(edge, tiles):
        put(a)
    pl.when(sides[1][0])(lambda: shift(1).start())
    for side in range(2):
        landing = pl.ds(0 if side == 0 else edge + tiles, edge)

        @pl.when(sides[side][0])
        def _():
            shift(side).wait_send()
            shift(1 - side).wait_recv()
            fresh_ref[landing] = halo[side]

        @pl.when(jnp.logical_not(sides[side][0]))
        def _():
            fresh_ref[landing] = jnp.zeros(halo.shape[1:], halo.dtype)


def normalise(gram, applied, total_points, edge, dtype, call_id):
    tiles, rank, points = applied.shape
    groups = digit_groups(lax.axis_size(AXES))
    widest = max(size for _, size in groups)
    sems = pltpu.SemaphoreType.DMA
    vmem = pl.BlockSpec(memory_space=pltpu.VMEM)
    return pl.pallas_call(
        functools.partial(norm_kernel, total_points, groups, edge),
        in_specs=[vmem, vmem],
        out_specs=vmem,
        out_shape=jax.ShapeDtypeStruct((tiles + 2 * edge, rank, points), dtype),
        scratch_shapes=[
            pltpu.VMEM((len(groups), rank, rank), jnp.float32),
            pltpu.VMEM((len(groups), widest, rank, rank), jnp.float32),
            pltpu.VMEM((2, max(edge, 1), rank, points), jnp.bfloat16),
            sems((len(groups), widest)),
            sems((len(groups), widest)),
            sems((2,)),
            sems((2,)),
        ],
        compiler_params=pltpu.CompilerParams(
            collective_id=call_id, has_side_effects=True, vmem_limit_bytes=40 * 1024 * 1024
        ),
    )(gram, applied)


def whole(shape):
    return pl.BlockSpec(shape, lambda i: (0,) * len(shape))


def per_tile(shape):
    return pl.BlockSpec((1,) + tuple(shape[1:]), lambda i: (i,) + (0,) * (len(shape) - 1))


def smem():
    return pl.BlockSpec(memory_space=pltpu.SMEM)


PARAMS = pltpu.CompilerParams(vmem_limit_bytes=40 * 1024 * 1024)


def window(own, edge):
    ahead = from_behind(own[:edge], -1)
    behind = from_behind(own[-edge:], 1)
    return behind, ahead


def local(members, initial, wet_counts, tile_coords, neighbours):
    tiles, count, points = members.shape
    rank = initial.shape[1]
    slots = neighbours.shape[1]
    edge = COLW + 2
    first_tile = lax.axis_index(AXES) * tiles
    total_points = float(tiles * lax.axis_size(AXES) * points)
    wet_mask = jnp.arange(points, dtype=jnp.int32)[None, :] < wet_counts[:, None]
    own_rows = jnp.where(wet_mask[:, None, :], members, jnp.zeros_like(members))
    join = lambda own, sides: jnp.concatenate([sides[0], own, sides[1]], 0)
    rows = join(own_rows, window(own_rows, edge))
    place = join(tile_coords, window(tile_coords, edge))
    current = join(initial, window(initial, edge))
    slot = jnp.where(neighbours >= 0, neighbours - (first_tile - edge), edge)
    slot = jnp.clip(slot, 0, tiles + 2 * edge - 1)
    delta = jnp.clip(place[slot] - tile_coords[:, None, :], -1, 1) + 1
    kind = jnp.where(neighbours >= 0, delta[..., 0] * 3 + delta[..., 1], 9)
    table = taper_table(points, 1.0 / (count - 1.0))
    turned = jnp.swapaxes(rows, 1, 2)
    applied_shape = jax.ShapeDtypeStruct((tiles, rank, points), jnp.float32)
    gram_shape = jax.ShapeDtypeStruct((rank, rank), jnp.float32)
    blocks_shape = jax.ShapeDtypeStruct((tiles, slots, points, points), jnp.bfloat16)
    blocks, applied, gram = pl.pallas_call(
        first_kernel,
        grid=(tiles,),
        in_specs=[
            smem(), smem(), whole(turned.shape), per_tile(own_rows.shape), whole(current.shape), whole(table.shape),
        ],
        out_specs=[per_tile(blocks_shape.shape), per_tile(applied_shape.shape), whole(gram_shape.shape)],
        out_shape=[blocks_shape, applied_shape, gram_shape],
        compiler_params=PARAMS,
    )(slot, kind, turned, own_rows, current, table)
    for sweep in range(ITERS):
        if sweep == ITERS - 1:
            return normalise(gram, applied, total_points, 0, jnp.float32, sweep)
        current = normalise(gram, applied, total_points, edge, jnp.bfloat16, sweep)
        applied, gram = pl.pallas_call(
            later_kernel,
            grid=(tiles,),
            in_specs=[smem(), whole(current.shape), per_tile(blocks.shape)],
            out_specs=[per_tile(applied_shape.shape), whole(gram_shape.shape)],
            out_shape=[applied_shape, gram_shape],
            compiler_params=PARAMS,
        )(slot, current, blocks)


def solution(mesh):
    spec = P(AXES, None, None)
    in_specs = (spec, spec, P(AXES), P(AXES, None), P(AXES, None))
    return jax.shard_map(local, mesh=mesh, in_specs=in_specs, out_specs=spec, check_vma=False)
```

```python
import functools

import jax
import jax.numpy as jnp
from jax import lax
from jax.experimental import pallas as pl
from jax.experimental.pallas import tpu as pltpu
from jax.sharding import PartitionSpec as P

TILE_SIDE = 16
COLW = 8
ITERS = 2
AXES = ("tiles", "rep")
HIGH = lax.Precision.HIGHEST


def gaspari(distance):
    scaled = distance / (0.5 * TILE_SIDE)
    clamped = jnp.maximum(scaled, 1.0)
    inner_part = (
        ((-0.25 * scaled + 0.5) * scaled + 0.625) * scaled - 5.0 / 3.0
    ) * scaled * scaled + 1.0
    outer_part = (
        ((((scaled / 12.0 - 0.5) * scaled + 0.625) * scaled + 5.0 / 3.0) * scaled - 5.0) * scaled
        + 4.0
        - 2.0 / (3.0 * clamped)
    )
    return jnp.where(scaled <= 1.0, inner_part, jnp.where(scaled <= 2.0, outer_part, 0.0))


def taper_at(step, points, scale):
    delta_x = step // 3 - 1
    delta_y = step % 3 - 1
    one = lax.broadcasted_iota(jnp.int32, (points, points), 0)
    two = lax.broadcasted_iota(jnp.int32, (points, points), 1)
    row = (delta_x * TILE_SIDE + one // TILE_SIDE - two // TILE_SIDE).astype(jnp.float32)
    col = (delta_y * TILE_SIDE + one % TILE_SIDE - two % TILE_SIDE).astype(jnp.float32)
    return gaspari(jnp.sqrt(row * row + col * col)) * scale


def open_kernel(
    edge, scale, wet_ref, members_ref, initial_ref, place_ref,
    own_ref, turned_ref, iter_ref, places_ref, table_ref,
    halo_rows, halo_iter, halo_place, send_sem, recv_sem,
):
    length = lax.axis_size(AXES)
    me = lax.axis_index(AXES[0]) * lax.axis_size(AXES[1]) + lax.axis_index(AXES[1])
    mesh_ids = pl.DeviceIdType.MESH
    barrier = pltpu.get_barrier_semaphore()
    sides = ((me > 0, -1), (me < length - 1, 1))
    for there, by in sides:

        @pl.when(there)
        def _():
            pl.semaphore_signal(barrier, inc=1, device_id=device_at(me + by), device_id_type=mesh_ids)

    tiles, count, points = members_ref.shape
    point = lax.broadcasted_iota(jnp.int32, (count, points), 1)
    for a in range(tiles):
        rows = members_ref[a].astype(jnp.float32)
        own_ref[a] = jnp.where(point < wet_ref[a], rows, 0.0).astype(jnp.bfloat16)
    pl.semaphore_wait(barrier, jnp.minimum(me, 1) + jnp.minimum(length - 1 - me, 1))

    pairs = ((own_ref, halo_rows), (initial_ref, halo_iter), (place_ref, halo_place))

    def shift(side, k):
        first = 0 if side == 0 else tiles - edge
        return pltpu.make_async_remote_copy(
            src_ref=pairs[k][0].at[pl.ds(first, edge)],
            dst_ref=pairs[k][1].at[1 - side],
            send_sem=send_sem.at[side, k],
            recv_sem=recv_sem.at[1 - side, k],
            device_id=device_at(me + sides[side][1]),
            device_id_type=mesh_ids,
        )

    for side in range(2):

        @pl.when(sides[side][0])
        def _():
            for k in range(3):
                shift(side, k).start()

    def turn(rows):
        return rows.astype(jnp.float32).T.astype(jnp.bfloat16)

    for a in range(tiles):
        turned_ref[edge + a] = turn(own_ref[a])
    iter_ref[pl.ds(edge, tiles)] = initial_ref[...]
    places_ref[pl.ds(edge, tiles)] = place_ref[...]

    @pl.loop(0, 9)
    def _(step):
        table_ref[step] = taper_at(step, points, scale)

    table_ref[9] = jnp.zeros((points, points), jnp.float32)

    for side in range(2):
        first = 0 if side == 0 else edge + tiles

        @pl.when(sides[side][0])
        def _():
            for k in range(3):
                shift(side, k).wait_send()
                shift(1 - side, k).wait_recv()
            for a in range(edge):
                turned_ref[first + a] = turn(halo_rows[side, a])
            iter_ref[pl.ds(first, edge)] = halo_iter[side]
            places_ref[pl.ds(first, edge)] = halo_place[side]

        @pl.when(jnp.logical_not(sides[side][0]))
        def _():
            turned_ref[pl.ds(first, edge)] = jnp.zeros((edge, points, count), jnp.bfloat16)
            iter_ref[pl.ds(first, edge)] = jnp.zeros(halo_iter.shape[1:], jnp.bfloat16)
            places_ref[pl.ds(first, edge)] = jnp.zeros(halo_place.shape[1:], jnp.int32)


def opening(members, initial, wet_counts, tile_coords, edge, call_id):
    tiles, count, points = members.shape
    rank = initial.shape[1]
    span = tiles + 2 * edge
    place = jnp.pad(tile_coords, ((0, 0), (0, 126)))[:, None, :]
    vmem = pl.BlockSpec(memory_space=pltpu.VMEM)
    return pl.pallas_call(
        functools.partial(open_kernel, edge, 1.0 / (count - 1.0)),
        in_specs=[smem(), vmem, vmem, vmem],
        out_specs=[vmem] * 5,
        out_shape=[
            jax.ShapeDtypeStruct(members.shape, jnp.bfloat16),
            jax.ShapeDtypeStruct((span, points, count), jnp.bfloat16),
            jax.ShapeDtypeStruct((span, rank, points), jnp.bfloat16),
            jax.ShapeDtypeStruct((span, 1, 128), jnp.int32),
            jax.ShapeDtypeStruct((10, points, points), jnp.float32),
        ],
        scratch_shapes=[
            pltpu.VMEM((2, edge, count, points), jnp.bfloat16),
            pltpu.VMEM((2, edge, rank, points), jnp.bfloat16),
            pltpu.VMEM((2, edge, 1, 128), jnp.int32),
            pltpu.SemaphoreType.DMA((2, 3)),
            pltpu.SemaphoreType.DMA((2, 3)),
        ],
        compiler_params=pltpu.CompilerParams(
            collective_id=call_id, has_side_effects=True, vmem_limit_bytes=40 * 1024 * 1024
        ),
    )(wet_counts, members, initial, place)


def gram_add(step, applied, gram_ref):
    part = lax.dot_general(
        applied, applied, (((1,), (1,)), ((), ())), precision=HIGH, preferred_element_type=jnp.float32
    )

    @pl.when(step == 0)
    def _():
        gram_ref[...] = part

    @pl.when(step != 0)
    def _():
        gram_ref[...] += part


def first_kernel(slot_ref, kind_ref, turned_ref, own_ref, iter_ref, table_ref, blocks_ref, applied_ref, gram_ref):
    step = pl.program_id(0)
    own = own_ref[0]
    total = None
    for s in range(slot_ref.shape[1]):
        at = slot_ref[step, s]
        product = jnp.dot(turned_ref[at], own, preferred_element_type=jnp.float32)
        block = (product * table_ref[kind_ref[step, s]]).astype(jnp.bfloat16)
        blocks_ref[0, s] = block
        part = jnp.dot(iter_ref[at], block, preferred_element_type=jnp.float32)
        total = part if total is None else total + part
    applied_ref[0] = total
    gram_add(step, total, gram_ref)


def later_kernel(slot_ref, iter_ref, blocks_ref, applied_ref, gram_ref):
    step = pl.program_id(0)
    total = None
    for s in range(slot_ref.shape[1]):
        part = jnp.dot(iter_ref[slot_ref[step, s]], blocks_ref[0, s], preferred_element_type=jnp.float32)
        total = part if total is None else total + part
    applied_ref[0] = total
    gram_add(step, total, gram_ref)


def device_at(index):
    width = lax.axis_size(AXES[1])
    return (index // width, index % width)


def digit_groups(length):
    groups = []
    stride = 1
    while stride < length:
        size = next(s for s in range(min(8, length // stride), 1, -1) if (length // stride) % s == 0)
        groups.append((stride, size))
        stride *= size
    return groups


def exchange(me, source, inbox, send_sem, recv_sem, groups):
    total = source[0]
    for phase, (stride, size) in enumerate(groups):
        digit = (me // stride) % size
        if phase:
            source[phase] = total
        inbox[phase, digit] = total
        copies = []
        for hop in range(1, size):
            other = me + ((digit + hop) % size - digit) * stride
            copy = pltpu.make_async_remote_copy(
                src_ref=source.at[phase],
                dst_ref=inbox.at[phase, digit],
                send_sem=send_sem.at[phase, hop],
                recv_sem=recv_sem.at[phase, hop],
                device_id=device_at(other),
                device_id_type=pl.DeviceIdType.MESH,
            )
            copy.start()
            copies.append(copy)
        for copy in copies:
            copy.wait()
        total = inbox[phase, 0]
        for at in range(1, size):
            total = total + inbox[phase, at]
    return total


def inverse_factor(left):
    rank = left.shape[0]
    rows = lax.broadcasted_iota(jnp.int32, (rank, rank), 0)
    cols = lax.broadcasted_iota(jnp.int32, (rank, rank), 1)
    work = jnp.concatenate([left, (rows == cols).astype(jnp.float32)], axis=1)
    down = lax.broadcasted_iota(jnp.int32, (rank, 1), 0)
    for j in range(rank):
        root = lax.sqrt(work[j : j + 1, j : j + 1])
        line = work[j : j + 1, :] / root
        factor = work[:, j : j + 1] / root
        work = jnp.where(down > j, work - factor * line, jnp.where(down == j, line, work))
    return work[:, rank:]


def norm_kernel(
    total_points, groups, edge, gram_ref, applied_ref, fresh_ref,
    source, inbox, halo, send_sem, recv_sem, halo_send, halo_recv,
):
    length = lax.axis_size(AXES)
    me = lax.axis_index(AXES[0]) * lax.axis_size(AXES[1]) + lax.axis_index(AXES[1])
    barrier = pltpu.get_barrier_semaphore()
    mesh_ids = pl.DeviceIdType.MESH
    greeted = 0
    for stride, size in groups:
        digit = (me // stride) % size
        for hop in range(1, size):
            other = me + ((digit + hop) % size - digit) * stride
            pl.semaphore_signal(barrier, inc=1, device_id=device_at(other), device_id_type=mesh_ids)
            greeted += 1
    sides = ((me > 0, -1), (me < length - 1, 1)) if edge else ()
    for there, by in sides:

        @pl.when(there)
        def _():
            pl.semaphore_signal(barrier, inc=1, device_id=device_at(me + by), device_id_type=mesh_ids)

    source[0] = gram_ref[...]
    if edge:
        greeted = greeted + jnp.minimum(me, 1) + jnp.minimum(length - 1 - me, 1)
    pl.semaphore_wait(barrier, greeted)

    inverse = inverse_factor(exchange(me, source, inbox, send_sem, recv_sem, groups) / total_points)
    tiles = applied_ref.shape[0]

    def put(a):
        fresh_ref[a + edge] = jnp.dot(
            inverse, applied_ref[a], precision=HIGH, preferred_element_type=jnp.float32
        ).astype(fresh_ref.dtype)

    if not edge:
        for a in range(tiles):
            put(a)
        return

    def shift(side):
        first = edge if side == 0 else tiles
        return pltpu.make_async_remote_copy(
            src_ref=fresh_ref.at[pl.ds(first, edge)],
            dst_ref=halo.at[1 - side],
            send_sem=halo_send.at[side],
            recv_sem=halo_recv.at[1 - side],
            device_id=device_at(me + sides[side][1]),
            device_id_type=mesh_ids,
        )

    for a in range(edge):
        put(a)
    pl.when(sides[0][0])(lambda: shift(0).start())
    for a in range(edge, tiles):
        put(a)
    pl.when(sides[1][0])(lambda: shift(1).start())
    for side in range(2):
        landing = pl.ds(0 if side == 0 else edge + tiles, edge)

        @pl.when(sides[side][0])
        def _():
            shift(side).wait_send()
            shift(1 - side).wait_recv()
            fresh_ref[landing] = halo[side]

        @pl.when(jnp.logical_not(sides[side][0]))
        def _():
            fresh_ref[landing] = jnp.zeros(halo.shape[1:], halo.dtype)


def normalise(gram, applied, total_points, edge, dtype, call_id):
    tiles, rank, points = applied.shape
    groups = digit_groups(lax.axis_size(AXES))
    widest = max(size for _, size in groups)
    sems = pltpu.SemaphoreType.DMA
    vmem = pl.BlockSpec(memory_space=pltpu.VMEM)
    return pl.pallas_call(
        functools.partial(norm_kernel, total_points, groups, edge),
        in_specs=[vmem, vmem],
        out_specs=vmem,
        out_shape=jax.ShapeDtypeStruct((tiles + 2 * edge, rank, points), dtype),
        scratch_shapes=[
            pltpu.VMEM((len(groups), rank, rank), jnp.float32),
            pltpu.VMEM((len(groups), widest, rank, rank), jnp.float32),
            pltpu.VMEM((2, max(edge, 1), rank, points), jnp.bfloat16),
            sems((len(groups), widest)),
            sems((len(groups), widest)),
            sems((2,)),
            sems((2,)),
        ],
        compiler_params=pltpu.CompilerParams(
            collective_id=call_id, has_side_effects=True, vmem_limit_bytes=40 * 1024 * 1024
        ),
    )(gram, applied)


def whole(shape):
    return pl.BlockSpec(shape, lambda i: (0,) * len(shape))


def per_tile(shape):
    return pl.BlockSpec((1,) + tuple(shape[1:]), lambda i: (i,) + (0,) * (len(shape) - 1))


def smem():
    return pl.BlockSpec(memory_space=pltpu.SMEM)


PARAMS = pltpu.CompilerParams(vmem_limit_bytes=40 * 1024 * 1024)


def local(members, initial, wet_counts, tile_coords, neighbours):
    tiles, count, points = members.shape
    rank = initial.shape[1]
    slots = neighbours.shape[1]
    edge = COLW + 2
    first_tile = lax.axis_index(AXES) * tiles
    total_points = float(tiles * lax.axis_size(AXES) * points)
    own_rows, turned, current, place, table = opening(
        members, initial, wet_counts, tile_coords, edge, ITERS
    )
    place = place[:, 0, :2]
    slot = jnp.where(neighbours >= 0, neighbours - (first_tile - edge), edge)
    slot = jnp.clip(slot, 0, tiles + 2 * edge - 1)
    delta = jnp.clip(place[slot] - tile_coords[:, None, :], -1, 1) + 1
    kind = jnp.where(neighbours >= 0, delta[..., 0] * 3 + delta[..., 1], 9)
    applied_shape = jax.ShapeDtypeStruct((tiles, rank, points), jnp.float32)
    gram_shape = jax.ShapeDtypeStruct((rank, rank), jnp.float32)
    blocks_shape = jax.ShapeDtypeStruct((tiles, slots, points, points), jnp.bfloat16)
    blocks, applied, gram = pl.pallas_call(
        first_kernel,
        grid=(tiles,),
        in_specs=[
            smem(), smem(), whole(turned.shape), per_tile(own_rows.shape), whole(current.shape), whole(table.shape),
        ],
        out_specs=[per_tile(blocks_shape.shape), per_tile(applied_shape.shape), whole(gram_shape.shape)],
        out_shape=[blocks_shape, applied_shape, gram_shape],
        compiler_params=PARAMS,
    )(slot, kind, turned, own_rows, current, table)
    for sweep in range(ITERS):
        if sweep == ITERS - 1:
            return normalise(gram, applied, total_points, 0, jnp.float32, sweep)
        current = normalise(gram, applied, total_points, edge, jnp.bfloat16, sweep)
        applied, gram = pl.pallas_call(
            later_kernel,
            grid=(tiles,),
            in_specs=[smem(), whole(current.shape), per_tile(blocks.shape)],
            out_specs=[per_tile(applied_shape.shape), whole(gram_shape.shape)],
            out_shape=[applied_shape, gram_shape],
            compiler_params=PARAMS,
        )(slot, current, blocks)


def solution(mesh):
    spec = P(AXES, None, None)
    in_specs = (spec, spec, P(AXES), P(AXES, None), P(AXES, None))
    return jax.shard_map(local, mesh=mesh, in_specs=in_specs, out_specs=spec, check_vma=False)
```

```python
import functools

import jax
import jax.numpy as jnp
from jax import lax
from jax.experimental import pallas as pl
from jax.experimental.pallas import tpu as pltpu
from jax.sharding import PartitionSpec as P

TILE_SIDE = 16
COLW = 8
ITERS = 2
AXES = ("tiles", "rep")
HIGH = lax.Precision.HIGHEST


def gaspari(distance):
    scaled = distance / (0.5 * TILE_SIDE)
    clamped = jnp.maximum(scaled, 1.0)
    inner_part = (
        ((-0.25 * scaled + 0.5) * scaled + 0.625) * scaled - 5.0 / 3.0
    ) * scaled * scaled + 1.0
    outer_part = (
        ((((scaled / 12.0 - 0.5) * scaled + 0.625) * scaled + 5.0 / 3.0) * scaled - 5.0) * scaled
        + 4.0
        - 2.0 / (3.0 * clamped)
    )
    return jnp.where(scaled <= 1.0, inner_part, jnp.where(scaled <= 2.0, outer_part, 0.0))


def taper_at(step, points, scale):
    delta_x = step // 3 - 1
    delta_y = step % 3 - 1
    one = lax.broadcasted_iota(jnp.int32, (points, points), 0)
    two = lax.broadcasted_iota(jnp.int32, (points, points), 1)
    row = (delta_x * TILE_SIDE + one // TILE_SIDE - two // TILE_SIDE).astype(jnp.float32)
    col = (delta_y * TILE_SIDE + one % TILE_SIDE - two % TILE_SIDE).astype(jnp.float32)
    return gaspari(jnp.sqrt(row * row + col * col)) * scale


def open_kernel(
    edge, scale, wet_ref, members_ref, initial_ref, place_ref,
    own_ref, turned_ref, iter_ref, places_ref, table_ref,
    halo_rows, halo_iter, halo_place, send_sem, recv_sem,
):
    length = lax.axis_size(AXES)
    me = lax.axis_index(AXES[0]) * lax.axis_size(AXES[1]) + lax.axis_index(AXES[1])
    mesh_ids = pl.DeviceIdType.MESH
    barrier = pltpu.get_barrier_semaphore()
    sides = ((me > 0, -1), (me < length - 1, 1))
    for there, by in sides:

        @pl.when(there)
        def _():
            pl.semaphore_signal(barrier, inc=1, device_id=device_at(me + by), device_id_type=mesh_ids)

    tiles, count, points = members_ref.shape
    point = lax.broadcasted_iota(jnp.int32, (count, points), 1)
    for a in range(tiles):
        rows = members_ref[a].astype(jnp.float32)
        own_ref[a] = jnp.where(point < wet_ref[a], rows, 0.0).astype(jnp.bfloat16)
    pl.semaphore_wait(barrier, jnp.minimum(me, 1) + jnp.minimum(length - 1 - me, 1))

    pairs = ((own_ref, halo_rows), (initial_ref, halo_iter), (place_ref, halo_place))

    def shift(side, k):
        first = 0 if side == 0 else tiles - edge
        return pltpu.make_async_remote_copy(
            src_ref=pairs[k][0].at[pl.ds(first, edge)],
            dst_ref=pairs[k][1].at[1 - side],
            send_sem=send_sem.at[side, k],
            recv_sem=recv_sem.at[1 - side, k],
            device_id=device_at(me + sides[side][1]),
            device_id_type=mesh_ids,
        )

    for side in range(2):

        @pl.when(sides[side][0])
        def _():
            for k in range(3):
                shift(side, k).start()

    def turn(rows):
        return rows.astype(jnp.float32).T.astype(jnp.bfloat16)

    for a in range(tiles):
        turned_ref[edge + a] = turn(own_ref[a])
    iter_ref[pl.ds(edge, tiles)] = initial_ref[...]
    places_ref[pl.ds(edge, tiles)] = place_ref[...]

    @pl.loop(0, 9)
    def _(step):
        table_ref[step] = taper_at(step, points, scale)

    table_ref[9] = jnp.zeros((points, points), jnp.float32)

    for side in range(2):
        first = 0 if side == 0 else edge + tiles

        @pl.when(sides[side][0])
        def _():
            for k in range(3):
                shift(side, k).wait_send()
                shift(1 - side, k).wait_recv()
            for a in range(edge):
                turned_ref[first + a] = turn(halo_rows[side, a])
            iter_ref[pl.ds(first, edge)] = halo_iter[side]
            places_ref[pl.ds(first, edge)] = halo_place[side]

        @pl.when(jnp.logical_not(sides[side][0]))
        def _():
            turned_ref[pl.ds(first, edge)] = jnp.zeros((edge, points, count), jnp.bfloat16)
            iter_ref[pl.ds(first, edge)] = jnp.zeros(halo_iter.shape[1:], jnp.bfloat16)
            places_ref[pl.ds(first, edge)] = jnp.zeros(halo_place.shape[1:], jnp.int32)


def opening(members, initial, wet_counts, tile_coords, edge, call_id):
    tiles, count, points = members.shape
    rank = initial.shape[1]
    span = tiles + 2 * edge
    place = jnp.pad(tile_coords, ((0, 0), (0, 126)))[:, None, :]
    vmem = pl.BlockSpec(memory_space=pltpu.VMEM)
    return pl.pallas_call(
        functools.partial(open_kernel, edge, 1.0 / (count - 1.0)),
        in_specs=[smem(), vmem, vmem, vmem],
        out_specs=[vmem] * 5,
        out_shape=[
            jax.ShapeDtypeStruct(members.shape, jnp.bfloat16),
            jax.ShapeDtypeStruct((span, points, count), jnp.bfloat16),
            jax.ShapeDtypeStruct((span, rank, points), jnp.bfloat16),
            jax.ShapeDtypeStruct((span, 1, 128), jnp.int32),
            jax.ShapeDtypeStruct((10, points, points), jnp.float32),
        ],
        scratch_shapes=[
            pltpu.VMEM((2, edge, count, points), jnp.bfloat16),
            pltpu.VMEM((2, edge, rank, points), jnp.bfloat16),
            pltpu.VMEM((2, edge, 1, 128), jnp.int32),
            pltpu.SemaphoreType.DMA((2, 3)),
            pltpu.SemaphoreType.DMA((2, 3)),
        ],
        compiler_params=pltpu.CompilerParams(
            collective_id=call_id, has_side_effects=True, vmem_limit_bytes=40 * 1024 * 1024
        ),
    )(wet_counts, members, initial, place)


def local_gram(applied_ref):
    total = None
    for a in range(applied_ref.shape[0]):
        applied = applied_ref[a]
        part = lax.dot_general(
            applied, applied, (((1,), (1,)), ((), ())), precision=HIGH, preferred_element_type=jnp.float32
        )
        total = part if total is None else total + part
    return total


def first_kernel(slot_ref, kind_ref, turned_ref, own_ref, iter_ref, table_ref, blocks_ref, applied_ref):
    step = pl.program_id(0)
    own = own_ref[0]
    total = None
    for s in range(slot_ref.shape[1]):
        at = slot_ref[step, s]
        product = jnp.dot(turned_ref[at], own, preferred_element_type=jnp.float32)
        block = (product * table_ref[kind_ref[step, s]]).astype(jnp.bfloat16)
        blocks_ref[0, s] = block
        part = jnp.dot(iter_ref[at], block, preferred_element_type=jnp.float32)
        total = part if total is None else total + part
    applied_ref[0] = total


def later_kernel(slot_ref, iter_ref, blocks_ref, applied_ref):
    step = pl.program_id(0)
    total = None
    for s in range(slot_ref.shape[1]):
        part = jnp.dot(iter_ref[slot_ref[step, s]], blocks_ref[0, s], preferred_element_type=jnp.float32)
        total = part if total is None else total + part
    applied_ref[0] = total


def device_at(index):
    width = lax.axis_size(AXES[1])
    return (index // width, index % width)


def digit_groups(length):
    groups = []
    stride = 1
    while stride < length:
        size = next(s for s in range(min(8, length // stride), 1, -1) if (length // stride) % s == 0)
        groups.append((stride, size))
        stride *= size
    return groups


def exchange(me, source, inbox, send_sem, recv_sem, groups):
    total = source[0]
    for phase, (stride, size) in enumerate(groups):
        digit = (me // stride) % size
        if phase:
            source[phase] = total
        inbox[phase, digit] = total
        copies = []
        for hop in range(1, size):
            other = me + ((digit + hop) % size - digit) * stride
            copy = pltpu.make_async_remote_copy(
                src_ref=source.at[phase],
                dst_ref=inbox.at[phase, digit],
                send_sem=send_sem.at[phase, hop],
                recv_sem=recv_sem.at[phase, hop],
                device_id=device_at(other),
                device_id_type=pl.DeviceIdType.MESH,
            )
            copy.start()
            copies.append(copy)
        for copy in copies:
            copy.wait()
        total = inbox[phase, 0]
        for at in range(1, size):
            total = total + inbox[phase, at]
    return total


def inverse_factor(left):
    rank = left.shape[0]
    rows = lax.broadcasted_iota(jnp.int32, (rank, rank), 0)
    cols = lax.broadcasted_iota(jnp.int32, (rank, rank), 1)
    work = jnp.concatenate([left, (rows == cols).astype(jnp.float32)], axis=1)
    down = lax.broadcasted_iota(jnp.int32, (rank, 1), 0)
    for j in range(rank):
        column = jnp.broadcast_to(work[:, j : j + 1], work.shape)
        line = work[j : j + 1, :] / column[j : j + 1, :]
        work = jnp.where(down > j, work - column * line, work)
    pivots = jnp.sum(jnp.where(rows == cols, work[:, :rank], 0.0), axis=1, keepdims=True)
    return work[:, rank:] / lax.sqrt(pivots)


def norm_kernel(
    total_points, groups, edge, applied_ref, fresh_ref,
    source, inbox, halo, send_sem, recv_sem, halo_send, halo_recv,
):
    length = lax.axis_size(AXES)
    me = lax.axis_index(AXES[0]) * lax.axis_size(AXES[1]) + lax.axis_index(AXES[1])
    barrier = pltpu.get_barrier_semaphore()
    mesh_ids = pl.DeviceIdType.MESH
    greeted = 0
    for stride, size in groups:
        digit = (me // stride) % size
        for hop in range(1, size):
            other = me + ((digit + hop) % size - digit) * stride
            pl.semaphore_signal(barrier, inc=1, device_id=device_at(other), device_id_type=mesh_ids)
            greeted += 1
    sides = ((me > 0, -1), (me < length - 1, 1)) if edge else ()
    for there, by in sides:

        @pl.when(there)
        def _():
            pl.semaphore_signal(barrier, inc=1, device_id=device_at(me + by), device_id_type=mesh_ids)

    source[0] = local_gram(applied_ref)
    if edge:
        greeted = greeted + jnp.minimum(me, 1) + jnp.minimum(length - 1 - me, 1)
    pl.semaphore_wait(barrier, greeted)

    inverse = inverse_factor(exchange(me, source, inbox, send_sem, recv_sem, groups) / total_points)
    tiles = applied_ref.shape[0]

    def put(a):
        fresh_ref[a + edge] = jnp.dot(
            inverse, applied_ref[a], precision=HIGH, preferred_element_type=jnp.float32
        ).astype(fresh_ref.dtype)

    if not edge:
        for a in range(tiles):
            put(a)
        return

    def shift(side):
        first = edge if side == 0 else tiles
        return pltpu.make_async_remote_copy(
            src_ref=fresh_ref.at[pl.ds(first, edge)],
            dst_ref=halo.at[1 - side],
            send_sem=halo_send.at[side],
            recv_sem=halo_recv.at[1 - side],
            device_id=device_at(me + sides[side][1]),
            device_id_type=mesh_ids,
        )

    for a in range(edge):
        put(a)
    pl.when(sides[0][0])(lambda: shift(0).start())
    for a in range(edge, tiles):
        put(a)
    pl.when(sides[1][0])(lambda: shift(1).start())
    for side in range(2):
        landing = pl.ds(0 if side == 0 else edge + tiles, edge)

        @pl.when(sides[side][0])
        def _():
            shift(side).wait_send()
            shift(1 - side).wait_recv()
            fresh_ref[landing] = halo[side]

        @pl.when(jnp.logical_not(sides[side][0]))
        def _():
            fresh_ref[landing] = jnp.zeros(halo.shape[1:], halo.dtype)


def normalise(applied, total_points, edge, dtype, call_id):
    tiles, rank, points = applied.shape
    groups = digit_groups(lax.axis_size(AXES))
    widest = max(size for _, size in groups)
    sems = pltpu.SemaphoreType.DMA
    vmem = pl.BlockSpec(memory_space=pltpu.VMEM)
    return pl.pallas_call(
        functools.partial(norm_kernel, total_points, groups, edge),
        in_specs=[vmem],
        out_specs=vmem,
        out_shape=jax.ShapeDtypeStruct((tiles + 2 * edge, rank, points), dtype),
        scratch_shapes=[
            pltpu.VMEM((len(groups), rank, rank), jnp.float32),
            pltpu.VMEM((len(groups), widest, rank, rank), jnp.float32),
            pltpu.VMEM((2, max(edge, 1), rank, points), jnp.bfloat16),
            sems((len(groups), widest)),
            sems((len(groups), widest)),
            sems((2,)),
            sems((2,)),
        ],
        compiler_params=pltpu.CompilerParams(
            collective_id=call_id, has_side_effects=True, vmem_limit_bytes=40 * 1024 * 1024
        ),
    )(applied)


def whole(shape):
    return pl.BlockSpec(shape, lambda i: (0,) * len(shape))


def per_tile(shape):
    return pl.BlockSpec((1,) + tuple(shape[1:]), lambda i: (i,) + (0,) * (len(shape) - 1))


def smem():
    return pl.BlockSpec(memory_space=pltpu.SMEM)


PARAMS = pltpu.CompilerParams(vmem_limit_bytes=40 * 1024 * 1024)


def local(members, initial, wet_counts, tile_coords, neighbours):
    tiles, count, points = members.shape
    rank = initial.shape[1]
    slots = neighbours.shape[1]
    edge = COLW + 2
    first_tile = lax.axis_index(AXES) * tiles
    total_points = float(tiles * lax.axis_size(AXES) * points)
    own_rows, turned, current, place, table = opening(
        members, initial, wet_counts, tile_coords, edge, ITERS
    )
    place = place[:, 0, :2]
    slot = jnp.where(neighbours >= 0, neighbours - (first_tile - edge), edge)
    slot = jnp.clip(slot, 0, tiles + 2 * edge - 1)
    delta = jnp.clip(place[slot] - tile_coords[:, None, :], -1, 1) + 1
    kind = jnp.where(neighbours >= 0, delta[..., 0] * 3 + delta[..., 1], 9)
    applied_shape = jax.ShapeDtypeStruct((tiles, rank, points), jnp.float32)
    blocks_shape = jax.ShapeDtypeStruct((tiles, slots, points, points), jnp.bfloat16)
    blocks, applied = pl.pallas_call(
        first_kernel,
        grid=(tiles,),
        in_specs=[
            smem(), smem(), whole(turned.shape), per_tile(own_rows.shape), whole(current.shape), whole(table.shape),
        ],
        out_specs=[per_tile(blocks_shape.shape), per_tile(applied_shape.shape)],
        out_shape=[blocks_shape, applied_shape],
        compiler_params=PARAMS,
    )(slot, kind, turned, own_rows, current, table)
    for sweep in range(ITERS):
        if sweep == ITERS - 1:
            return normalise(applied, total_points, 0, jnp.float32, sweep)
        current = normalise(applied, total_points, edge, jnp.bfloat16, sweep)
        applied = pl.pallas_call(
            later_kernel,
            grid=(tiles,),
            in_specs=[smem(), whole(current.shape), per_tile(blocks.shape)],
            out_specs=per_tile(applied_shape.shape),
            out_shape=applied_shape,
            compiler_params=PARAMS,
        )(slot, current, blocks)


def solution(mesh):
    spec = P(AXES, None, None)
    in_specs = (spec, spec, P(AXES), P(AXES, None), P(AXES, None))
    return jax.shard_map(local, mesh=mesh, in_specs=in_specs, out_specs=spec, check_vma=False)
```
